128 devices in a mesh: head: 4 (over y_lo, core), blk: 32 (over x, y_hi, z).
Axes of the slice: x: 4, y: 4 (y_hi: 2, y_lo: 2; y = y_hi * 2 + y_lo), z: 4, core: 2. Of those that a mesh axis runs over, the one named last changes fastest.
Arguments:
- x_ckpt: bfloat16 [32768, 5120], P(('blk', 'head')), may hold values from -6 to 6
- w_query: bfloat16 [5120, 2560], P('blk', 'head'), may hold values from -0.078125 to 0.078125
- w_key: bfloat16 [5120, 512], P('blk', 'head'), may hold values from -0.078125 to 0.078125
- w_value: bfloat16 [5120, 512], P('blk', 'head'), may hold values from -0.078125 to 0.078125
- dout_seq: bfloat16 [32768, 2560], P(('blk', 'head')), may hold values from -192 to 192
- out_heads: bfloat16 [32768, 2560], P('blk', 'head'), may hold values from -4 to 4
- lse_heads: float32 [32768, 20], P('blk', 'head'), may hold values from 6.5 to 9
- span_order: int32 [256], replicated, may hold values from 0 to 255, each once
Outputs:
- grad_query: bfloat16 [32768, 2560], P(('blk', 'head'))
- grad_key: bfloat16 [32768, 512], P(('blk', 'head'))
- grad_value: bfloat16 [32768, 512], P(('blk', 'head'))
The draws below stay inside these ranges and needn't reach their ends.
Inputs may be any that keep to these rules, and one draw needn't show every extreme that they name: `span_order`: each span number appears once.
All inputs are finite; a program needn't handle non-finite values.
Results may differ from the reference program's by a relative error of at most 0.018.
The reference program's roundings to bfloat16 on the way (of `query`, `prob_half` and `grad_score`) count: a program that leaves them out, or rounds other values in their place, can miss the bound.
Values may be sent and summed in bfloat16 or wider, within the bound.
No kernel may reach another device: no remote copies, remote signals or barrier semaphores. Data moves between devices by JAX's collectives and lax.ppermute only.
A program may use at most 128 MiB of HBM per device.

```python
import jax
import jax.numpy as jnp
from jax import lax

D = 5120
HQ = 20
HK = 4
HD = 128
TD = 256
REACH = 2
GROUP = 5
SEQ = 32768
NCHUNK = 256
N_HEAD = 4
N_BLK = 32


def level_of(rng, dims, pieces, low, largest):
    def one(dim, blocks):
        draws = jax.random.uniform(jax.random.fold_in(jax.random.fold_in(rng, 6), dim), (blocks,), jnp.float32, low / len(pieces), largest / len(pieces))
        return jnp.repeat(jnp.exp(draws), dims[dim] // blocks).reshape((-1,) + (1,) * (len(dims) - dim - 1))

    factor_of = one(*pieces[0])
    for cut in pieces[1:]:
        factor_of = factor_of * one(*cut)
    return factor_of


def bell_draw(rng, dims, scale, limit, split=(), held_as=jnp.bfloat16):
    entries = scale * jax.random.normal(rng, dims, jnp.float32)
    if split:
        entries = entries * level_of(rng, dims, split, -0.22, 0.18)
    return jnp.clip(entries, -limit, limit).astype(held_as)


def setup_inputs(seed: int = 0) -> dict:
    splits = jax.random.split(jax.random.key(seed), 9)
    return {
        "x_ckpt": bell_draw(splits[0], (SEQ, D), 1.0, 6.0, ((0, 128),)),
        "w_query": bell_draw(splits[1], (D, HQ * HD), D ** -0.5, 0.078125, ((0, 32), (1, 4))),
        "w_key": bell_draw(splits[2], (D, HK * HD), D ** -0.5, 0.078125, ((0, 32), (1, 4))),
        "w_value": bell_draw(splits[3], (D, HK * HD), D ** -0.5, 0.078125, ((0, 32), (1, 4))),
        "dout_seq": bell_draw(splits[4], (SEQ, HQ * HD), 32.0, 192.0, ((0, 128),)),
        "out_heads": bell_draw(splits[5], (SEQ, HQ * HD), 0.3, 4.0, ((0, 32), (1, 4))),
        "lse_heads": jnp.clip(6.5 + 2.5 * jax.random.uniform(splits[6], (SEQ, HQ), jnp.float32) ** level_of(splits[6], (SEQ, HQ), ((0, 32), (1, 4)), -0.2, 0.2), 6.5, 9.0),
        "span_order": jax.random.permutation(splits[7], NCHUNK).astype(jnp.int32),
    }


def token_positions(span_order):
    span_len = TD // 2
    index = jnp.arange(SEQ, dtype=jnp.int32)
    return span_order[index // span_len] * span_len + index % span_len


def tile_grads(query, grad_out, lse_rows, delta_rows, query_pos, keys, values, key_pos):
    group_len = query.shape[0]
    scale = HD ** -0.5
    query_f = query.astype(jnp.float32).reshape(group_len, HQ, HD)
    grad_f = grad_out.astype(jnp.float32).reshape(group_len, HQ, HD)
    keys_f = jnp.repeat(keys.astype(jnp.float32).reshape(group_len, HK, HD), GROUP, axis=1)
    values_f = jnp.repeat(values.astype(jnp.float32).reshape(group_len, HK, HD), GROUP, axis=1)
    visible = key_pos[None, :] <= query_pos[:, None]
    score = jnp.einsum("qhd,khd->hqk", query_f, keys_f) * scale
    attn_prob = jnp.where(visible[None], jnp.exp(score - lse_rows.T[:, :, None]), 0.0)
    prob_half = lax.optimization_barrier(attn_prob.astype(jnp.bfloat16)).astype(jnp.float32)
    grad_values = jnp.einsum("hqk,qhd->khd", prob_half, grad_f)
    grad_values = grad_values.reshape(group_len, HK, GROUP, HD).sum(axis=2).reshape(group_len, HK * HD)
    grad_prob = jnp.einsum("qhd,khd->hqk", grad_f, values_f)
    grad_score = attn_prob * (grad_prob - delta_rows.T[:, :, None]) * scale
    score_half = lax.optimization_barrier(grad_score.astype(jnp.bfloat16)).astype(jnp.float32)
    grad_query = jnp.einsum("hqk,khd->qhd", score_half, keys_f).reshape(group_len, HQ * HD)
    grad_keys = jnp.einsum("hqk,qhd->khd", score_half, query_f)
    grad_keys = grad_keys.reshape(group_len, HK, GROUP, HD).sum(axis=2).reshape(group_len, HK * HD)
    return grad_query, grad_keys, grad_values


def reference(x_ckpt, w_query, w_key, w_value, dout_seq, out_heads, lse_heads, span_order):
    query = jnp.dot(x_ckpt, w_query, preferred_element_type=jnp.float32).astype(jnp.bfloat16)
    keys = jnp.dot(x_ckpt, w_key, preferred_element_type=jnp.float32).astype(jnp.bfloat16)
    values = jnp.dot(x_ckpt, w_value, preferred_element_type=jnp.float32).astype(jnp.bfloat16)
    delta = jnp.sum((dout_seq.astype(jnp.float32) * out_heads.astype(jnp.float32)).reshape(SEQ, HQ, HD), axis=2)
    positions = token_positions(span_order)
    group_len = N_HEAD * TD

    def take(array, group):
        return lax.dynamic_slice_in_dim(array, (group * group_len).astype(jnp.int32), group_len, 0)

    def per_group(block):
        grad_q = jnp.zeros((group_len, HQ * HD), jnp.float32)
        key_list = []
        value_list = []
        for distance in range(REACH + 1):
            other = (block - distance) % N_BLK
            part_q, part_k, part_v = tile_grads(take(query, block), take(dout_seq, block), take(lse_heads, block), take(delta, block), take(positions, block), take(keys, other), take(values, other), take(positions, other))
            grad_q = grad_q + part_q
            key_list.append(part_k)
            value_list.append(part_v)
        return grad_q, jnp.stack(key_list), jnp.stack(value_list)

    q_blocks, k_blocks, v_blocks = lax.map(per_group, jnp.arange(N_BLK, dtype=jnp.int32))
    k_total = jnp.zeros((N_BLK, group_len, HK * HD), jnp.float32)
    v_total = jnp.zeros((N_BLK, group_len, HK * HD), jnp.float32)
    for distance in range(REACH + 1):
        k_total = k_total + jnp.roll(k_blocks[:, distance], -distance, axis=0)
        v_total = v_total + jnp.roll(v_blocks[:, distance], -distance, axis=0)
    grad_query = q_blocks.reshape(SEQ, HQ * HD).astype(jnp.bfloat16)
    grad_key = k_total.reshape(SEQ, HK * HD).astype(jnp.bfloat16)
    grad_value = v_total.reshape(SEQ, HK * HD).astype(jnp.bfloat16)
    return grad_query, grad_key, grad_value
```

```python
import jax
import jax.numpy as jnp
from jax import lax
from jax.experimental import pallas as pl
from jax.experimental.pallas import tpu as pltpu
from jax.sharding import Mesh, PartitionSpec as P

HD = 128
SPAN = 128
REACH = 2
HEAD = ("y_lo", "core")
BLK = ("x", "y_hi", "z")
FINE = (2, 2, 4, 2, 4)
SCALE = HD ** (-0.5)
LOG2E = 1.4426950408889634
BIG = 1e30
NN = (((1,), (0,)), ((), ()))
NT = (((1,), (1,)), ((), ()))


def dot(a, b, dims):
    return lax.dot_general(a, b, dims, preferred_element_type=jnp.float32)


def tile_grads(query, grad_out, lse2, delta, query_spans, key_spans, kvs, own, key_rows, query_rows):
    rows, cols = query.shape
    heads = cols // HD
    n = len(kvs)
    length = kvs[0].shape[0]
    query_rows = min(query_rows, rows)

    def body(qspan_ref, kspan_ref, q_ref, g_ref, lse_ref, delta_ref, *rest):
        kv_refs, dq_ref, dkv_refs, kt_ref = rest[:n], rest[n], rest[n + 1 : 2 * n + 1], rest[2 * n + 1]

        @pl.when(pl.program_id(0) == 0)
        def _():
            for i in range(n):
                dkv_refs[i][...] = jnp.zeros_like(dkv_refs[i])
                kt_ref[i] = kv_refs[i][:, :HD].T

        lane = lax.broadcasted_iota(jnp.int32, (1, query_rows), 1)
        spans = query_rows // SPAN
        for qb in range(rows // query_rows):
            qs = pl.ds(qb * query_rows, query_rows)
            q, g = q_ref[qs, :], g_ref[qs, :]
            lse, delt = lse_ref[0, :, qs], delta_ref[0, :, qs]
            qspan = jnp.full((1, query_rows), qspan_ref[qb * spans], jnp.int32)
            for s in range(1, spans):
                qspan = jnp.where(lane >= s * SPAN, qspan_ref[qb * spans + s], qspan)
            qpos = qspan * SPAN + lane % SPAN
            dq = None
            for i in range(n):
                for kb in range(length // key_rows):
                    ks = pl.ds(kb * key_rows, key_rows)
                    score = dot(kv_refs[i][ks, :HD], q, NT)
                    gprob = dot(kv_refs[i][ks, HD:], g, NT)
                    probs, scores = [], []
                    for s in range(key_rows // SPAN):
                        at = slice(s * SPAN, (s + 1) * SPAN)
                        kspan = kspan_ref[i, kb * (key_rows // SPAN) + s]
                        if i == own:
                            kpos = kspan * SPAN + lax.broadcasted_iota(jnp.int32, (SPAN, 1), 0)
                            prob = jnp.exp2(
                                jnp.where(kpos <= qpos, score[at] * (SCALE * LOG2E) - lse, -BIG)
                            )
                        else:
                            prob = jnp.exp2(
                                score[at] * (SCALE * LOG2E) - jnp.where(kspan < qspan, lse, BIG)
                            )
                        probs.append(prob.astype(jnp.bfloat16))
                        scores.append((prob * (gprob[at] - delt)).astype(jnp.bfloat16))
                    prob_half = jnp.concatenate(probs, 0)
                    score_half = jnp.concatenate(scores, 0)
                    dkv_refs[i][ks, HD:] += dot(prob_half, g, NN)
                    dkv_refs[i][ks, :HD] += dot(score_half, q, NN) * SCALE
                    part = dot(kt_ref[i, :, ks], score_half, NN)
                    dq = part if dq is None else dq + part
            dq_ref[qs, :] = dq.T * SCALE

    def whole(shape):
        return pl.BlockSpec(shape, lambda h: (0,) * len(shape))

    smem = pl.BlockSpec(memory_space=pltpu.SMEM)
    per_head = pl.BlockSpec((rows, HD), lambda h: (0, h))
    per_row = pl.BlockSpec((1, 1, rows), lambda h: (h, 0, 0))
    return pl.pallas_call(
        body,
        grid=(heads,),
        in_specs=[smem, smem, per_head, per_head, per_row, per_row] + [whole((length, 2 * HD))] * n,
        out_specs=[per_head] + [whole((length, 2 * HD))] * n,
        out_shape=[jax.ShapeDtypeStruct((rows, cols), jnp.float32)]
        + [jax.ShapeDtypeStruct((length, 2 * HD), jnp.float32)] * n,
        scratch_shapes=[pltpu.VMEM((n, HD, length), jnp.bfloat16)],
        compiler_params=pltpu.CompilerParams(
            vmem_limit_bytes=48 * 2**20, dimension_semantics=("arbitrary",)
        ),
        cost_estimate=pl.CostEstimate(
            flops=10 * rows * length * n * cols,
            bytes_accessed=n * length * HD * 12 + rows * cols * 8,
            transcendentals=rows * length * n * heads,
        ),
    )(query_spans, key_spans, query, grad_out, lse2, delta, *kvs)


def shift(block, axis, by):
    size = lax.axis_size(axis)
    return lax.ppermute(block, axis, [(i, (i + by) % size) for i in range(size)])


def to_peer(block, d):
    return lax.ppermute(block, HEAD, [(i, i ^ d) for i in range(4)]) if d else block


def local(x_ckpt, w_query, w_key, w_value, dout_seq, out_heads, lse_heads, span_order):
    rows = x_ckpt.shape[0]
    cols = w_query.shape[1]
    heads = cols // HD
    me = lax.axis_index(HEAD)
    group = lax.axis_index(BLK)
    groups = lax.axis_size(BLK)
    peers = range(4)
    mine = [me ^ d for d in peers]

    w_own = jnp.concatenate([w_key, w_value, w_query], axis=1)
    w_all = lax.all_gather(w_own, BLK, axis=0, tiled=True)

    x_pair = to_peer(x_ckpt, 2)
    x_rows = jnp.concatenate([x_ckpt, to_peer(x_ckpt, 1), x_pair, to_peer(x_pair, 1)], axis=0)

    grad_out = jnp.concatenate(
        [
            to_peer(lax.dynamic_slice_in_dim(dout_seq, mine[d] * cols, cols, 1), d)
            for d in peers
        ],
        axis=0,
    )

    def by_peer(array):
        return jnp.concatenate(
            [lax.dynamic_slice_in_dim(array, mine[d] * rows, rows, 0) for d in peers], axis=0
        )

    lse2 = (by_peer(lse_heads) * LOG2E).T[:, None, :]
    delta = jnp.sum(
        (grad_out.astype(jnp.float32) * by_peer(out_heads).astype(jnp.float32)).reshape(
            4 * rows, heads, HD
        ),
        axis=2,
    ).T[:, None, :]

    spans = rows // SPAN

    def spans_of(which):
        base = which * (4 * spans)
        return jnp.concatenate(
            [lax.dynamic_slice_in_dim(span_order, base + mine[d] * spans, spans) for d in peers]
        )

    span_ids = [spans_of((group - r) % groups) for r in range(REACH + 1)]

    kv = dot(x_rows, w_all[:, : 2 * HD], NN).astype(jnp.bfloat16)
    query = dot(x_rows, w_all[:, 2 * HD :], NN).astype(jnp.bfloat16)

    kv1, kv2 = shift(kv, BLK, 1), shift(kv, BLK, 2)
    far = slice(2 * rows, None)
    near = slice(0, 2 * rows)

    def part(at, kvs, ids, own):
        spans_at = slice(at.start // SPAN, None if at.stop is None else at.stop // SPAN)
        return tile_grads(
            query[at], grad_out[at], lse2[:, :, at], delta[:, :, at],
            span_ids[0][spans_at], jnp.stack(ids), kvs, own, 1024, 256,
        )

    dq_far0, dkv0_far = part(far, [kv], [span_ids[0]], 0)
    dq_far1, dkv1_far, dkv2_far = part(far, [kv1, kv2], span_ids[1:], -1)
    dq_far = (dq_far0 + dq_far1).astype(jnp.bfloat16)
    dq2, dq3 = to_peer(dq_far[:rows], 2), to_peer(dq_far[rows:], 3)
    dq_near1, dkv1_near, dkv2_near = part(near, [kv1, kv2], span_ids[1:], -1)
    back1 = shift((dkv1_far + dkv1_near).astype(jnp.bfloat16), BLK, -1)
    back2 = shift((dkv2_far + dkv2_near).astype(jnp.bfloat16), BLK, -2)
    dq_near0, dkv0_near = part(near, [kv], [span_ids[0]], 0)
    dq_near = (dq_near0 + dq_near1).astype(jnp.bfloat16)
    dq1 = to_peer(dq_near[rows:], 1)
    dkv = (
        dkv0_far + dkv0_near + back1.astype(jnp.float32) + back2.astype(jnp.float32)
    ).astype(jnp.bfloat16)
    dkvs = [to_peer(dkv[d * rows : (d + 1) * rows], d) for d in peers]
    dqs = [dq_near[:rows], dq1, dq2, dq3]

    def by_head(pieces):
        width = pieces[0].shape[1]
        out = jnp.zeros((rows, 4 * width), jnp.bfloat16)
        for d in peers:
            out = lax.dynamic_update_slice_in_dim(out, pieces[d], mine[d] * width, 1)
        return out

    return (
        by_head(dqs),
        by_head([piece[:, :HD] for piece in dkvs]),
        by_head([piece[:, HD:] for piece in dkvs]),
    )


def solution(mesh):
    fine = Mesh(mesh.devices.reshape(FINE), HEAD + BLK)
    rows = P(BLK + HEAD, None)
    both = P(BLK, HEAD)
    return jax.shard_map(
        local,
        mesh=fine,
        in_specs=(rows, both, both, both, rows, both, both, P()),
        out_specs=(rows, rows, rows),
        check_vma=False,
    )
```

```python
import jax
import jax.numpy as jnp
from jax import lax
from jax.experimental import pallas as pl
from jax.experimental.pallas import tpu as pltpu
from jax.sharding import Mesh, PartitionSpec as P

HD = 128
SPAN = 128
REACH = 2
HEAD = ("y_lo", "core")
BLK = ("x", "y_hi", "z")
FINE = (2, 2, 4, 2, 4)
SCALE = HD ** (-0.5)
LOG2E = 1.4426950408889634
BIG = 1e30
NN = (((1,), (0,)), ((), ()))
NT = (((1,), (1,)), ((), ()))


def dot(a, b, dims):
    return lax.dot_general(a, b, dims, preferred_element_type=jnp.float32)


def tile_grads(query, grad_out, lse2, delta, query_spans, key_spans, kvs, own, dq_sum, dkv_sums, dq_type, dkv_type):
    rows, cols = query.shape
    heads = cols // HD
    n = len(kvs)
    length = kvs[0].shape[0]
    query_rows = min(256, rows)
    key_rows = length
    sums = ([] if dq_sum is None else [dq_sum]) + ([] if dkv_sums is None else list(dkv_sums))

    def body(qspan_ref, kspan_ref, q_ref, g_ref, lse_ref, delta_ref, *rest):
        kv_refs, rest = rest[:n], list(rest[n:])
        dq_sum_ref = rest.pop(0) if dq_sum is not None else None
        dkv_sum_refs = [rest.pop(0) for _ in range(n)] if dkv_sums is not None else None
        dq_ref, dkv_refs, kt_ref, total = rest[0], rest[1 : n + 1], rest[n + 1], rest[n + 2]

        @pl.when(pl.program_id(0) == 0)
        def _():
            for i in range(n):
                if dkv_sums is None:
                    total[i] = jnp.zeros((length, 2 * HD), jnp.float32)
                else:
                    total[i] = dkv_sum_refs[i][...]
                kt_ref[i] = kv_refs[i][:, :HD].T

        lane = lax.broadcasted_iota(jnp.int32, (1, query_rows), 1)
        spans = query_rows // SPAN
        for qb in range(rows // query_rows):
            qs = pl.ds(qb * query_rows, query_rows)
            q, g = q_ref[qs, :], g_ref[qs, :]
            lse, delt = lse_ref[0, :, qs], delta_ref[0, :, qs]
            qspan = jnp.full((1, query_rows), qspan_ref[qb * spans], jnp.int32)
            for s in range(1, spans):
                qspan = jnp.where(lane >= s * SPAN, qspan_ref[qb * spans + s], qspan)
            qpos = qspan * SPAN + lane % SPAN
            dq = None
            for i in range(n):
                for kb in range(length // key_rows):
                    ks = pl.ds(kb * key_rows, key_rows)
                    score = dot(kv_refs[i][ks, :HD], q, NT)
                    gprob = dot(kv_refs[i][ks, HD:], g, NT)
                    probs, scores = [], []
                    for s in range(key_rows // SPAN):
                        at = slice(s * SPAN, (s + 1) * SPAN)
                        kspan = kspan_ref[i, kb * (key_rows // SPAN) + s]
                        if i == own:
                            kpos = kspan * SPAN + lax.broadcasted_iota(jnp.int32, (SPAN, 1), 0)
                            prob = jnp.exp2(
                                jnp.where(kpos <= qpos, score[at] * (SCALE * LOG2E) - lse, -BIG)
                            )
                        else:
                            prob = jnp.exp2(
                                score[at] * (SCALE * LOG2E) - jnp.where(kspan < qspan, lse, BIG)
                            )
                        probs.append(prob.astype(jnp.bfloat16))
                        scores.append((prob * (gprob[at] - delt)).astype(jnp.bfloat16))
                    prob_half = jnp.concatenate(probs, 0)
                    score_half = jnp.concatenate(scores, 0)
                    total[i, ks, HD:] += dot(prob_half, g, NN)
                    total[i, ks, :HD] += dot(score_half, q, NN) * SCALE
                    part = dot(kt_ref[i, :, ks], score_half, NN)
                    dq = part if dq is None else dq + part
            dq = dq.T * SCALE
            if dq_sum is not None:
                dq = dq + dq_sum_ref[qs, :]
            dq_ref[qs, :] = dq.astype(dq_type)

        @pl.when(pl.program_id(0) == heads - 1)
        def _():
            for i in range(n):
                dkv_refs[i][...] = total[i].astype(dkv_type)

    def whole(shape):
        return pl.BlockSpec(shape, lambda h: (0,) * len(shape))

    smem = pl.BlockSpec(memory_space=pltpu.SMEM)
    per_head = pl.BlockSpec((rows, HD), lambda h: (0, h))
    per_row = pl.BlockSpec((1, 1, rows), lambda h: (h, 0, 0))
    sum_specs = ([] if dq_sum is None else [per_head]) + (
        [] if dkv_sums is None else [whole((length, 2 * HD))] * n
    )
    return pl.pallas_call(
        body,
        grid=(heads,),
        in_specs=[smem, smem, per_head, per_head, per_row, per_row]
        + [whole((length, 2 * HD))] * n
        + sum_specs,
        out_specs=[per_head] + [whole((length, 2 * HD))] * n,
        out_shape=[jax.ShapeDtypeStruct((rows, cols), dq_type)]
        + [jax.ShapeDtypeStruct((length, 2 * HD), dkv_type)] * n,
        scratch_shapes=[
            pltpu.VMEM((n, HD, length), jnp.bfloat16),
            pltpu.VMEM((n, length, 2 * HD), jnp.float32),
        ],
        compiler_params=pltpu.CompilerParams(
            vmem_limit_bytes=32 * 2**20, dimension_semantics=("arbitrary",)
        ),
        cost_estimate=pl.CostEstimate(
            flops=10 * rows * length * n * cols,
            bytes_accessed=n * length * HD * 12 + rows * cols * 8,
            transcendentals=rows * length * n * heads,
        ),
    )(query_spans, key_spans, query, grad_out, lse2, delta, *kvs, *sums)


def prepare(pieces, out_heads, mine):
    rows, cols = pieces[0].shape
    heads = cols // HD

    def body(mine_ref, *refs):
        out_ref, grad_ref, delta_ref = refs[4:]
        for d in range(4):
            at = pl.ds(d * rows, rows)
            there = pl.ds(pl.multiple_of(mine_ref[d] * rows, rows), rows)
            grad_ref[at, :] = refs[d][...]
            for h in range(heads):
                cs = slice(h * HD, (h + 1) * HD)
                product = refs[d][:, cs].astype(jnp.float32) * out_ref[there, cs].astype(jnp.float32)
                delta_ref[h, :, at] = jnp.sum(product.T, axis=0, keepdims=True)

    vmem = pl.BlockSpec(memory_space=pltpu.VMEM)
    return pl.pallas_call(
        body,
        in_specs=[pl.BlockSpec(memory_space=pltpu.SMEM)] + [vmem] * 5,
        out_specs=[vmem, vmem],
        out_shape=[
            jax.ShapeDtypeStruct((4 * rows, cols), jnp.bfloat16),
            jax.ShapeDtypeStruct((heads, 1, 4 * rows), jnp.float32),
        ],
        compiler_params=pltpu.CompilerParams(vmem_limit_bytes=24 * 2**20),
        cost_estimate=pl.CostEstimate(
            flops=8 * rows * cols, bytes_accessed=24 * rows * cols, transcendentals=0
        ),
    )(mine, *pieces, out_heads)


def by_head(pieces, mine, widths):
    rows = pieces[0].shape[0]
    n = len(widths)

    def body(mine_ref, *refs):
        for d in range(4):
            at = 0
            for out_ref, width in zip(refs[4:], widths):
                to = pl.ds(pl.multiple_of(mine_ref[d] * width, HD), width)
                out_ref[:, to] = refs[d][:, at : at + width]
                at += width

    vmem = pl.BlockSpec(memory_space=pltpu.VMEM)
    return pl.pallas_call(
        body,
        in_specs=[pl.BlockSpec(memory_space=pltpu.SMEM)] + [vmem] * 4,
        out_specs=[vmem] * n,
        out_shape=[jax.ShapeDtypeStruct((rows, 4 * width), jnp.bfloat16) for width in widths],
        cost_estimate=pl.CostEstimate(
            flops=0, bytes_accessed=16 * rows * sum(widths), transcendentals=0
        ),
    )(mine, *pieces)


def shift(block, axis, by):
    size = lax.axis_size(axis)
    return lax.ppermute(block, axis, [(i, (i + by) % size) for i in range(size)])


def to_peer(block, d):
    return lax.ppermute(block, HEAD, [(i, i ^ d) for i in range(4)]) if d else block


def fence(*arrays):
    return lax.optimization_barrier(arrays)


def gather(blocks):
    half = blocks[0].shape[0] // 2
    axes = (("z", "x"), ("x", "z"))

    def step(sends):
        got = fence(*(shift(array, axis, by) for array, axis, by in sends))
        return list(zip(got[0::2], got[1::2]))

    block = [
        jnp.concatenate([b[s * half : (s + 1) * half] for b in blocks], axis=0) for s in range(2)
    ]
    near = step([(block[s], axes[s][0], by) for s in range(2) for by in (1, 3)])
    far = step(
        [
            (piece, axes[s][0], by)
            for s in range(2)
            for by, piece in ((1, near[s][0][:half]), (3, near[s][1][half:]))
        ]
    )
    line = [
        jnp.concatenate([block[s], near[s][0], far[s][0], far[s][1], near[s][1]], axis=0)
        for s in range(2)
    ]
    near = step([(line[s], axes[s][1], by) for s in range(2) for by in (1, 3)])
    far = step(
        [
            (piece, axes[s][1], by)
            for s in range(2)
            for by, piece in ((1, near[s][0][: 4 * half]), (3, near[s][1][4 * half :]))
        ]
    )
    return [[line[s], near[s][0], far[s][0], far[s][1], near[s][1]] for s in range(2)]


def lines_place(half):
    def copies(px, py, pz):
        for dx in range(4):
            for other in range(2):
                for dz in range(4):
                    for side, (first, second) in enumerate(((dz, dx), (dx, dz))):
                        src = (first * 2 + other) * half
                        kind = (0, 1, 2, 4)[second]
                        if second == 2 and first >= 2:
                            kind, src = 3, src - 4 * half
                        row = ((((px + 4 - dx) % 4) * 2 + (py + other) % 2) * 4 + (pz + 4 - dz) % 4)
                        yield dx, side * 5 + kind, src, row * (2 * half) + side * half, half

    return copies


def planes_place(length):
    def copies(px, py, pz):
        for dx in range(4):
            ax = (px + 4 - dx) % 4
            for z in range(4):
                for other in range(2):
                    src = ((ax * 4 + z) * 2 + other) * length
                    yield dx, 0, src, ((ax * 2 + (py + other) % 2) * 4 + z) * length, length

    return copies


def project(x_pieces, w_place, w_pieces, where):
    depth = x_pieces[0].shape[1]
    width = w_pieces[0].shape[1]
    chunk = depth // 4
    rows = sum(piece.shape[0] for piece in x_pieces)
    n_x, n_w = len(x_pieces), len(w_pieces)
    at_once = 512

    def body(where_ref, *refs):
        x_refs, w_refs = refs[:n_x], refs[n_x : n_x + n_w]
        out_ref, x_mem, w_mem, total, x_sems, w_sems = refs[n_x + n_w :]
        px, py, pz = where_ref[0], where_ref[1], where_ref[2]

        def columns(dx):
            return pl.ds(pl.multiple_of(((px + 4 - dx) % 4) * chunk, 128), chunk)

        moves = list(w_place(px, py, pz))
        for dx in range(4):
            for which, src, dst, size in [m[1:] for m in moves if m[0] == dx]:
                src = src if isinstance(src, int) else pl.multiple_of(src, 16)
                pltpu.make_async_copy(
                    w_refs[which].at[pl.ds(src, size), :],
                    w_mem.at[pl.ds(pl.multiple_of(dst, 16), size), :],
                    w_sems.at[dx],
                ).start()
            at = 0
            for ref in x_refs:
                pltpu.make_async_copy(
                    ref.at[:, columns(dx)],
                    x_mem.at[pl.ds(at, ref.shape[0]), columns(dx)],
                    x_sems.at[dx],
                ).start()
                at += ref.shape[0]
        for dx in range(4):
            here = columns(dx)
            pltpu.make_async_copy(w_mem.at[here, :], w_mem.at[here, :], w_sems.at[dx]).wait()
            pltpu.make_async_copy(x_mem.at[:, here], x_mem.at[:, here], x_sems.at[dx]).wait()
            for start in range(0, rows, at_once):
                at = pl.ds(start, at_once)
                part = dot(x_mem[at, here], w_mem[here, :], NN)
                if dx == 0:
                    total[at, :] = part
                elif dx == 3:
                    out_ref[at, :] = (total[at, :] + part).astype(jnp.bfloat16)
                else:
                    total[at, :] += part

    hbm = pl.BlockSpec(memory_space=pl.ANY)
    return pl.pallas_call(
        body,
        in_specs=[pl.BlockSpec(memory_space=pltpu.SMEM)] + [hbm] * (n_x + n_w),
        out_specs=pl.BlockSpec(memory_space=pltpu.VMEM),
        out_shape=jax.ShapeDtypeStruct((rows, width), jnp.bfloat16),
        scratch_shapes=[
            pltpu.VMEM((rows, depth), jnp.bfloat16),
            pltpu.VMEM((depth, width), jnp.bfloat16),
            pltpu.VMEM((rows, width), jnp.float32),
            pltpu.SemaphoreType.DMA((4,)),
            pltpu.SemaphoreType.DMA((4,)),
        ],
        compiler_params=pltpu.CompilerParams(vmem_limit_bytes=32 * 2**20),
        cost_estimate=pl.CostEstimate(
            flops=2 * rows * depth * width,
            bytes_accessed=2 * (rows * depth + depth * width + rows * width),
            transcendentals=0,
        ),
    )(where, *x_pieces, *w_pieces)


def local(x_ckpt, w_query, w_key, w_value, dout_seq, out_heads, lse_heads, span_order):
    rows = x_ckpt.shape[0]
    cols = w_query.shape[1]
    me = lax.axis_index(HEAD)
    group = lax.axis_index(BLK)
    groups = lax.axis_size(BLK)
    peers = range(4)
    mine = [me ^ d for d in peers]
    mine_all = jnp.stack(mine)
    where = jnp.stack([lax.axis_index(axis) for axis in ("x", "y_hi", "z")])

    w_own = jnp.concatenate([w_key, w_value, w_query], axis=1)
    w_pair = shift(w_own, "y_hi", 1)
    q_rows = jnp.concatenate([w_query, w_pair[:, 2 * HD :]], axis=0)
    q_weights = lax.all_gather(q_rows, ("x", "z"), axis=0, tiled=True)
    kv_lines = gather([w_own[:, : 2 * HD], w_pair[:, : 2 * HD]])

    x_sent, _ = fence(x_ckpt, w_pair)
    x_far = to_peer(x_sent, 2)
    x_core = to_peer(x_sent, 1)
    x_far, *flat = fence(x_far, *kv_lines[0], *kv_lines[1])
    kv_lines = [flat[:5], flat[5:]]
    x_pieces = [x_ckpt, x_core, x_far, to_peer(x_far, 1)]

    lse_rows = lse_heads.T * LOG2E
    lse2 = jnp.concatenate(
        [lax.dynamic_slice_in_dim(lse_rows, mine[d] * rows, rows, 1) for d in peers], axis=1
    )[:, None, :]
    spans = rows // SPAN

    def spans_of(which):
        base = which * (4 * spans)
        return jnp.concatenate(
            [lax.dynamic_slice_in_dim(span_order, base + mine[d] * spans, spans) for d in peers]
        )

    span_ids = [spans_of((group - r) % groups) for r in range(REACH + 1)]

    kv = project(x_pieces, lines_place(w_own.shape[0] // 2), kv_lines[0] + kv_lines[1], where)
    kv1, kv2 = shift(kv, BLK, 1), shift(kv, BLK, 2)
    grads = [lax.dynamic_slice_in_dim(dout_seq, mine[d] * cols, cols, 1) for d in peers]
    *grads, _ = fence(*grads, x_far)
    grads = [to_peer(grads[d], d) for d in peers]
    query = project(x_pieces, planes_place(w_query.shape[0]), [q_weights], where)
    *grads, query = fence(*grads, query)
    grad_out, delta = prepare(grads, out_heads, mine_all)

    far = slice(2 * rows, 4 * rows)
    near = slice(0, 2 * rows)

    def part(at, kvs, ids, own, dq_sum, dkv_sums, dq_type, dkv_type):
        return tile_grads(
            query[at], grad_out[at], lse2[:, :, at], delta[:, :, at],
            span_ids[0][at.start // SPAN : at.stop // SPAN], jnp.stack(ids), kvs, own,
            dq_sum, dkv_sums, dq_type, dkv_type,
        )

    f32, bf16 = jnp.float32, jnp.bfloat16
    dq_far, dkv0 = part(far, [kv], span_ids[:1], 0, None, None, f32, f32)
    dq_far, dkv1, dkv2 = part(far, [kv1, kv2], span_ids[1:], -1, dq_far, None, bf16, f32)
    dq_near, dkv1, dkv2 = part(near, [kv1, kv2], span_ids[1:], -1, None, [dkv1, dkv2], f32, bf16)
    dq2, dq3 = to_peer(dq_far[:rows], 2), to_peer(dq_far[rows:], 3)
    back1, back2 = shift(dkv1, BLK, -1), shift(dkv2, BLK, -2)
    dq_near, dkv0 = part(near, [kv], span_ids[:1], 0, dq_near, [dkv0], bf16, f32)
    dq1 = to_peer(dq_near[rows:], 1)
    dkv = (dkv0 + back1.astype(f32) + back2.astype(f32)).astype(bf16)
    dkvs = [to_peer(dkv[d * rows : (d + 1) * rows], d) for d in peers]
    (grad_query,) = by_head([dq_near[:rows], dq1, dq2, dq3], mine_all, [cols])
    grad_key, grad_value = by_head(dkvs, mine_all, [HD, HD])
    return grad_query, grad_key, grad_value


def solution(mesh):
    fine = Mesh(mesh.devices.reshape(FINE), HEAD + BLK)
    rows = P(BLK + HEAD, None)
    both = P(BLK, HEAD)
    return jax.shard_map(
        local,
        mesh=fine,
        in_specs=(rows, both, both, both, rows, both, both, P()),
        out_specs=(rows, rows, rows),
        check_vma=False,
    )
```

```python
import jax
import jax.numpy as jnp
from jax import lax
from jax.experimental import pallas as pl
from jax.experimental.pallas import tpu as pltpu
from jax.sharding import Mesh, PartitionSpec as P

HD = 128
SPAN = 128
REACH = 2
HEAD = ("y_lo", "core")
BLK = ("x", "y_hi", "z")
FINE = (2, 2, 4, 2, 4)
SCALE = HD ** (-0.5)
LOG2E = 1.4426950408889634
BIG = 1e30
NN = (((1,), (0,)), ((), ()))
NT = (((1,), (1,)), ((), ()))


def dot(a, b, dims):
    return lax.dot_general(a, b, dims, preferred_element_type=jnp.float32)


def tile_grads(start, rows, query, grad_out, lse2, delta, query_spans, key_spans, kvs, own, dq_sum, dkv_sums, dq_type, dkv_type):
    cols = query.shape[1]
    heads = cols // HD
    n = len(kvs)
    length = kvs[0].shape[0]
    query_rows = min(256, rows)
    block = start // rows
    key_rows = length
    sums = ([] if dq_sum is None else [dq_sum]) + ([] if dkv_sums is None else list(dkv_sums))

    def body(qspan_ref, kspan_ref, q_ref, g_ref, lse_ref, delta_ref, *rest):
        kv_refs, rest = rest[:n], list(rest[n:])
        dq_sum_ref = rest.pop(0) if dq_sum is not None else None
        dkv_sum_refs = [rest.pop(0) for _ in range(n)] if dkv_sums is not None else None
        dq_ref, dkv_refs, kt_ref, total = rest[0], rest[1 : n + 1], rest[n + 1], rest[n + 2]

        @pl.when(pl.program_id(0) == 0)
        def _():
            for i in range(n):
                if dkv_sums is None:
                    total[i] = jnp.zeros((length, 2 * HD), jnp.float32)
                else:
                    total[i] = dkv_sum_refs[i][...]
                kt_ref[i] = kv_refs[i][:, :HD].T

        lane = lax.broadcasted_iota(jnp.int32, (1, query_rows), 1)
        spans = query_rows // SPAN
        for qb in range(rows // query_rows):
            qs = pl.ds(qb * query_rows, query_rows)
            q, g = q_ref[qs, :], g_ref[qs, :]
            lse, delt = lse_ref[0, :, qs], delta_ref[0, :, qs]
            qspan = jnp.full((1, query_rows), qspan_ref[start // SPAN + qb * spans], jnp.int32)
            for s in range(1, spans):
                qspan = jnp.where(lane >= s * SPAN, qspan_ref[start // SPAN + qb * spans + s], qspan)
            qpos = qspan * SPAN + lane % SPAN
            dq = None
            for i in range(n):
                for kb in range(length // key_rows):
                    ks = pl.ds(kb * key_rows, key_rows)
                    score = dot(kv_refs[i][ks, :HD], q, NT)
                    gprob = dot(kv_refs[i][ks, HD:], g, NT)
                    probs, scores = [], []
                    for s in range(key_rows // SPAN):
                        at = slice(s * SPAN, (s + 1) * SPAN)
                        kspan = kspan_ref[i, kb * (key_rows // SPAN) + s]
                        if i == own:
                            kpos = kspan * SPAN + lax.broadcasted_iota(jnp.int32, (SPAN, 1), 0)
                            prob = jnp.exp2(
                                jnp.where(kpos <= qpos, score[at] * (SCALE * LOG2E) - lse, -BIG)
                            )
                        else:
                            prob = jnp.exp2(
                                score[at] * (SCALE * LOG2E) - jnp.where(kspan < qspan, lse, BIG)
                            )
                        probs.append(prob.astype(jnp.bfloat16))
                        scores.append((prob * (gprob[at] - delt)).astype(jnp.bfloat16))
                    prob_half = jnp.concatenate(probs, 0)
                    score_half = jnp.concatenate(scores, 0)
                    total[i, ks, HD:] += dot(prob_half, g, NN)
                    total[i, ks, :HD] += dot(score_half, q, NN) * SCALE
                    part = dot(kt_ref[i, :, ks], score_half, NN)
                    dq = part if dq is None else dq + part
            dq = dq.T * SCALE
            if dq_sum is not None:
                dq = dq + dq_sum_ref[qs, :]
            dq_ref[qs, :] = dq.astype(dq_type)

        @pl.when(pl.program_id(0) == heads - 1)
        def _():
            for i in range(n):
                dkv_refs[i][...] = total[i].astype(dkv_type)

    def whole(shape):
        return pl.BlockSpec(shape, lambda h: (0,) * len(shape))

    smem = pl.BlockSpec(memory_space=pltpu.SMEM)
    per_head = pl.BlockSpec((rows, HD), lambda h: (block, h))
    per_row = pl.BlockSpec((1, 1, rows), lambda h: (h, 0, block))
    out_head = pl.BlockSpec((rows, HD), lambda h: (0, h))
    sum_head = out_head if dq_sum is not None and dq_sum.shape[0] == rows else per_head
    sum_specs = ([] if dq_sum is None else [sum_head]) + (
        [] if dkv_sums is None else [whole((length, 2 * HD))] * n
    )
    return pl.pallas_call(
        body,
        grid=(heads,),
        in_specs=[smem, smem, per_head, per_head, per_row, per_row]
        + [whole((length, 2 * HD))] * n
        + sum_specs,
        out_specs=[out_head] + [whole((length, 2 * HD))] * n,
        out_shape=[jax.ShapeDtypeStruct((rows, cols), dq_type)]
        + [jax.ShapeDtypeStruct((length, 2 * HD), dkv_type)] * n,
        scratch_shapes=[
            pltpu.VMEM((n, HD, length), jnp.bfloat16),
            pltpu.VMEM((n, length, 2 * HD), jnp.float32),
        ],
        compiler_params=pltpu.CompilerParams(
            vmem_limit_bytes=32 * 2**20, dimension_semantics=("arbitrary",)
        ),
        cost_estimate=pl.CostEstimate(
            flops=10 * rows * length * n * cols,
            bytes_accessed=n * length * HD * 12 + rows * cols * 8,
            transcendentals=rows * length * n * heads,
        ),
    )(query_spans, key_spans, query, grad_out, lse2, delta, *kvs, *sums)


def prepare(pieces, out_heads, mine):
    rows, cols = pieces[0].shape
    heads = cols // HD

    def body(mine_ref, *refs):
        out_ref, grad_ref, delta_ref = refs[4:]
        for d in range(4):
            at = pl.ds(d * rows, rows)
            there = pl.ds(pl.multiple_of(mine_ref[d] * rows, rows), rows)
            grad_ref[at, :] = refs[d][...]
            for h in range(heads):
                cs = slice(h * HD, (h + 1) * HD)
                product = refs[d][:, cs].astype(jnp.float32) * out_ref[there, cs].astype(jnp.float32)
                delta_ref[h, :, at] = jnp.sum(product.T, axis=0, keepdims=True)

    vmem = pl.BlockSpec(memory_space=pltpu.VMEM)
    return pl.pallas_call(
        body,
        in_specs=[pl.BlockSpec(memory_space=pltpu.SMEM)] + [vmem] * 5,
        out_specs=[vmem, vmem],
        out_shape=[
            jax.ShapeDtypeStruct((4 * rows, cols), jnp.bfloat16),
            jax.ShapeDtypeStruct((heads, 1, 4 * rows), jnp.float32),
        ],
        compiler_params=pltpu.CompilerParams(vmem_limit_bytes=24 * 2**20),
        cost_estimate=pl.CostEstimate(
            flops=8 * rows * cols, bytes_accessed=24 * rows * cols, transcendentals=0
        ),
    )(mine, *pieces, out_heads)


def by_head(pieces, mine, widths):
    rows = pieces[0].shape[0]
    n = len(widths)

    def body(mine_ref, *refs):
        for d in range(4):
            at = 0
            for out_ref, width in zip(refs[4:], widths):
                to = pl.ds(pl.multiple_of(mine_ref[d] * width, HD), width)
                out_ref[:, to] = refs[d][:, at : at + width]
                at += width

    vmem = pl.BlockSpec(memory_space=pltpu.VMEM)
    return pl.pallas_call(
        body,
        in_specs=[pl.BlockSpec(memory_space=pltpu.SMEM)] + [vmem] * 4,
        out_specs=[vmem] * n,
        out_shape=[jax.ShapeDtypeStruct((rows, 4 * width), jnp.bfloat16) for width in widths],
        cost_estimate=pl.CostEstimate(
            flops=0, bytes_accessed=16 * rows * sum(widths), transcendentals=0
        ),
    )(mine, *pieces)


def shift(block, axis, by):
    size = lax.axis_size(axis)
    return lax.ppermute(block, axis, [(i, (i + by) % size) for i in range(size)])


def to_peer(block, d):
    return lax.ppermute(block, HEAD, [(i, i ^ d) for i in range(4)]) if d else block


def fence(*arrays):
    return lax.optimization_barrier(arrays)


def gather(blocks):
    half = blocks[0].shape[0] // 2
    axes = (("z", "x"), ("x", "z"))

    def step(sends):
        got = fence(*(shift(array, axis, by) for array, axis, by in sends))
        return list(zip(got[0::2], got[1::2]))

    block = [
        jnp.concatenate([b[s * half : (s + 1) * half] for b in blocks], axis=0) for s in range(2)
    ]
    near = step([(block[s], axes[s][0], by) for s in range(2) for by in (1, 3)])
    far = step(
        [
            (piece, axes[s][0], by)
            for s in range(2)
            for by, piece in ((1, near[s][0][:half]), (3, near[s][1][half:]))
        ]
    )
    line = [
        jnp.concatenate([block[s], near[s][0], far[s][0], far[s][1], near[s][1]], axis=0)
        for s in range(2)
    ]
    near = step([(line[s], axes[s][1], by) for s in range(2) for by in (1, 3)])
    far = step(
        [
            (piece, axes[s][1], by)
            for s in range(2)
            for by, piece in ((1, near[s][0][: 4 * half]), (3, near[s][1][4 * half :]))
        ]
    )
    return [[line[s], near[s][0], far[s][0], far[s][1], near[s][1]] for s in range(2)]


def lines_place(half):
    def copies(px, py, pz):
        for dx in range(4):
            for other in range(2):
                for dz in range(4):
                    for side, (first, second) in enumerate(((dz, dx), (dx, dz))):
                        src = (first * 2 + other) * half
                        kind = (0, 1, 2, 4)[second]
                        if second == 2 and first >= 2:
                            kind, src = 3, src - 4 * half
                        row = ((((px + 4 - dx) % 4) * 2 + (py + other) % 2) * 4 + (pz + 4 - dz) % 4)
                        yield dx, side * 5 + kind, src, row * (2 * half) + side * half, half

    return copies


def planes_place(length):
    def copies(px, py, pz):
        for dx in range(4):
            ax = (px + 4 - dx) % 4
            for z in range(4):
                for other in range(2):
                    src = ((ax * 4 + z) * 2 + other) * length
                    yield dx, 0, src, ((ax * 2 + (py + other) % 2) * 4 + z) * length, length

    return copies


def project(x_pieces, w_place, w_pieces, where):
    depth = x_pieces[0].shape[1]
    width = w_pieces[0].shape[1]
    chunk = depth // 4
    rows = sum(piece.shape[0] for piece in x_pieces)
    n_x, n_w = len(x_pieces), len(w_pieces)
    at_once = 512

    def body(where_ref, *refs):
        x_refs, w_refs = refs[:n_x], refs[n_x : n_x + n_w]
        out_ref, x_mem, w_mem, total, x_sems, w_sems = refs[n_x + n_w :]
        px, py, pz = where_ref[0], where_ref[1], where_ref[2]

        def columns(dx):
            return pl.ds(pl.multiple_of(((px + 4 - dx) % 4) * chunk, 128), chunk)

        moves = list(w_place(px, py, pz))
        for dx in range(4):
            for which, src, dst, size in [m[1:] for m in moves if m[0] == dx]:
                src = src if isinstance(src, int) else pl.multiple_of(src, 16)
                pltpu.make_async_copy(
                    w_refs[which].at[pl.ds(src, size), :],
                    w_mem.at[pl.ds(pl.multiple_of(dst, 16), size), :],
                    w_sems.at[dx],
                ).start()
            at = 0
            for ref in x_refs:
                pltpu.make_async_copy(
                    ref.at[:, columns(dx)],
                    x_mem.at[pl.ds(at, ref.shape[0]), columns(dx)],
                    x_sems.at[dx],
                ).start()
                at += ref.shape[0]
        for dx in range(4):
            here = columns(dx)
            pltpu.make_async_copy(w_mem.at[here, :], w_mem.at[here, :], w_sems.at[dx]).wait()
            pltpu.make_async_copy(x_mem.at[:, here], x_mem.at[:, here], x_sems.at[dx]).wait()
            for start in range(0, rows, at_once):
                at = pl.ds(start, at_once)
                part = dot(x_mem[at, here], w_mem[here, :], NN)
                if dx == 0:
                    total[at, :] = part
                elif dx == 3:
                    out_ref[at, :] = (total[at, :] + part).astype(jnp.bfloat16)
                else:
                    total[at, :] += part

    hbm = pl.BlockSpec(memory_space=pltpu.HBM)
    return pl.pallas_call(
        body,
        in_specs=[pl.BlockSpec(memory_space=pltpu.SMEM)] + [hbm] * (n_x + n_w),
        out_specs=pl.BlockSpec(memory_space=pltpu.VMEM),
        out_shape=jax.ShapeDtypeStruct((rows, width), jnp.bfloat16),
        scratch_shapes=[
            pltpu.VMEM((rows, depth), jnp.bfloat16),
            pltpu.VMEM((depth, width), jnp.bfloat16),
            pltpu.VMEM((rows, width), jnp.float32),
            pltpu.SemaphoreType.DMA((4,)),
            pltpu.SemaphoreType.DMA((4,)),
        ],
        compiler_params=pltpu.CompilerParams(vmem_limit_bytes=56 * 2**20),
        cost_estimate=pl.CostEstimate(
            flops=2 * rows * depth * width,
            bytes_accessed=2 * (rows * depth + depth * width + rows * width),
            transcendentals=0,
        ),
    )(where, *x_pieces, *w_pieces)


def local(x_ckpt, w_query, w_key, w_value, dout_seq, out_heads, lse_heads, span_order):
    rows = x_ckpt.shape[0]
    cols = w_query.shape[1]
    me = lax.axis_index(HEAD)
    group = lax.axis_index(BLK)
    groups = lax.axis_size(BLK)
    peers = range(4)
    mine = [me ^ d for d in peers]
    mine_all = jnp.stack(mine)
    where = jnp.stack([lax.axis_index(axis) for axis in ("x", "y_hi", "z")])

    w_own = jnp.concatenate([w_key, w_value, w_query], axis=1)
    w_pair = shift(w_own, "y_hi", 1)
    q_rows = jnp.concatenate([w_query, w_pair[:, 2 * HD :]], axis=0)
    q_weights = lax.all_gather(q_rows, ("x", "z"), axis=0, tiled=True)
    kv_lines = gather([w_own[:, : 2 * HD], w_pair[:, : 2 * HD]])

    x_sent, _ = fence(x_ckpt, w_pair)
    x_far = to_peer(x_sent, 2)
    x_core = to_peer(x_sent, 1)
    x_far, *flat = fence(x_far, *kv_lines[0], *kv_lines[1])
    kv_lines = [flat[:5], flat[5:]]
    x_pieces = [x_ckpt, x_core, x_far, to_peer(x_far, 1)]

    lse_rows = lse_heads.T * LOG2E
    lse2 = jnp.concatenate(
        [lax.dynamic_slice_in_dim(lse_rows, mine[d] * rows, rows, 1) for d in peers], axis=1
    )[:, None, :]
    spans = rows // SPAN

    def spans_of(which):
        base = which * (4 * spans)
        return jnp.concatenate(
            [lax.dynamic_slice_in_dim(span_order, base + mine[d] * spans, spans) for d in peers]
        )

    span_ids = [spans_of((group - r) % groups) for r in range(REACH + 1)]

    kv = project(x_pieces, lines_place(w_own.shape[0] // 2), kv_lines[0] + kv_lines[1], where)
    kv1 = shift(kv, BLK, 1)
    grads = [lax.dynamic_slice_in_dim(dout_seq, mine[d] * cols, cols, 1) for d in peers]
    *grads, _ = fence(*grads, x_far)
    grads = [to_peer(grads[d], d) for d in peers]
    query = project(x_pieces, planes_place(w_query.shape[0]), [q_weights], where)
    *grads, kv1, query = fence(*grads, kv1, query)
    kv2 = shift(kv1, BLK, 1)
    grad_out, delta = prepare(grads, out_heads, mine_all)

    def part(start, count, keys, ids, own, dq_sum, dkv_sum, dq_type, dkv_type):
        return tile_grads(
            start, count, query, grad_out, lse2, delta, span_ids[0], ids[None], [keys], own,
            dq_sum, None if dkv_sum is None else [dkv_sum], dq_type, dkv_type,
        )

    f32, bf16 = jnp.float32, jnp.bfloat16
    half = 2 * rows
    dq, dkv1 = part(0, 4 * rows, kv1, span_ids[1], -1, None, None, f32, bf16)
    back1 = shift(dkv1, BLK, -1)
    dq, dkv2 = part(0, 4 * rows, kv2, span_ids[2], -1, dq, None, f32, bf16)
    back2 = shift(dkv2, BLK, -2)
    dq_far, dkv0 = part(half, half, kv, span_ids[0], 0, dq, None, bf16, f32)
    dq2, dq3 = to_peer(dq_far[:rows], 2), to_peer(dq_far[rows:], 3)
    dq_near, dkv0 = part(0, half, kv, span_ids[0], 0, dq, dkv0, bf16, f32)
    dq1 = to_peer(dq_near[rows:], 1)
    dkv = (dkv0 + back1.astype(f32) + back2.astype(f32)).astype(bf16)
    dkv, dq2, dq3 = fence(dkv, dq2, dq3)
    dkvs = [to_peer(dkv[d * rows : (d + 1) * rows], d) for d in peers]
    (grad_query,) = by_head([dq_near[:rows], dq1, dq2, dq3], mine_all, [cols])
    grad_key, grad_value = by_head(dkvs, mine_all, [HD, HD])
    return grad_query, grad_key, grad_value


def solution(mesh):
    fine = Mesh(mesh.devices.reshape(FINE), HEAD + BLK)
    rows = P(BLK + HEAD, None)
    both = P(BLK, HEAD)
    return jax.shard_map(
        local,
        mesh=fine,
        in_specs=(rows, both, both, both, rows, both, both, P()),
        out_specs=(rows, rows, rows),
        check_vma=False,
    )
```

```python
import jax
import jax.numpy as jnp
from jax import lax
from jax.experimental import pallas as pl
from jax.experimental.pallas import tpu as pltpu
from jax.sharding import Mesh, PartitionSpec as P

HD = 128
SPAN = 128
REACH = 2
HEAD = ("y_lo", "core")
BLK = ("x", "y_hi", "z")
FINE = (2, 2, 4, 2, 4)
SCALE = HD ** (-0.5)
LOG2E = 1.4426950408889634
BIG = 1e30
NN = (((1,), (0,)), ((), ()))
NT = (((1,), (1,)), ((), ()))


def dot(a, b, dims):
    return lax.dot_general(a, b, dims, preferred_element_type=jnp.float32)


def tile_grads(start, rows, query, grad_out, lse2, delta, query_spans, key_spans, kvs, own, dq_sum, dkv_sums, dq_type, dkv_type):
    cols = query.shape[1]
    heads = cols // HD
    n = len(kvs)
    length = kvs[0].shape[0]
    query_rows = min(256, rows)
    block = start // rows
    key_rows = length
    sums = ([] if dq_sum is None else [dq_sum]) + ([] if dkv_sums is None else list(dkv_sums))

    def body(qspan_ref, kspan_ref, q_ref, g_ref, lse_ref, delta_ref, *rest):
        kv_refs, rest = rest[:n], list(rest[n:])
        dq_sum_ref = rest.pop(0) if dq_sum is not None else None
        dkv_sum_refs = [rest.pop(0) for _ in range(n)] if dkv_sums is not None else None
        dq_ref, dkv_refs, kt_ref, total = rest[0], rest[1 : n + 1], rest[n + 1], rest[n + 2]

        @pl.when(pl.program_id(0) == 0)
        def _():
            for i in range(n):
                if dkv_sums is None:
                    total[i] = jnp.zeros((length, 2 * HD), jnp.float32)
                else:
                    total[i] = dkv_sum_refs[i][...]
                kt_ref[i] = kv_refs[i][:, :HD].T

        lane = lax.broadcasted_iota(jnp.int32, (1, query_rows), 1)
        spans = query_rows // SPAN
        for qb in range(rows // query_rows):
            qs = pl.ds(qb * query_rows, query_rows)
            q, g = q_ref[qs, :], g_ref[qs, :]
            lse, delt = lse_ref[0, :, qs], delta_ref[0, :, qs]
            qspan = jnp.full((1, query_rows), qspan_ref[start // SPAN + qb * spans], jnp.int32)
            for s in range(1, spans):
                qspan = jnp.where(lane >= s * SPAN, qspan_ref[start // SPAN + qb * spans + s], qspan)
            qpos = qspan * SPAN + lane % SPAN
            dq = None
            for i in range(n):
                for kb in range(length // key_rows):
                    ks = pl.ds(kb * key_rows, key_rows)
                    score = dot(kv_refs[i][ks, :HD], q, NT)
                    gprob = dot(kv_refs[i][ks, HD:], g, NT)
                    probs, scores = [], []
                    for s in range(key_rows // SPAN):
                        at = slice(s * SPAN, (s + 1) * SPAN)
                        kspan = kspan_ref[i, kb * (key_rows // SPAN) + s]
                        if i == own:
                            kpos = kspan * SPAN + lax.broadcasted_iota(jnp.int32, (SPAN, 1), 0)
                            prob = jnp.exp2(
                                jnp.where(kpos <= qpos, score[at] * (SCALE * LOG2E) - lse, -BIG)
                            )
                        else:
                            prob = jnp.exp2(
                                score[at] * (SCALE * LOG2E) - jnp.where(kspan < qspan, lse, BIG)
                            )
                        probs.append(prob.astype(jnp.bfloat16))
                        scores.append((prob * (gprob[at] - delt)).astype(jnp.bfloat16))
                    prob_half = jnp.concatenate(probs, 0)
                    score_half = jnp.concatenate(scores, 0)
                    total[i, ks, HD:] += dot(prob_half, g, NN)
                    total[i, ks, :HD] += dot(score_half, q, NN) * SCALE
                    part = dot(kt_ref[i, :, ks], score_half, NN)
                    dq = part if dq is None else dq + part
            dq = dq.T * SCALE
            if dq_sum is not None:
                dq = dq + dq_sum_ref[qs, :]
            dq_ref[qs, :] = dq.astype(dq_type)

        @pl.when(pl.program_id(0) == heads - 1)
        def _():
            for i in range(n):
                dkv_refs[i][...] = total[i].astype(dkv_type)

    def whole(shape):
        return pl.BlockSpec(shape, lambda h: (0,) * len(shape))

    smem = pl.BlockSpec(memory_space=pltpu.SMEM)
    per_head = pl.BlockSpec((rows, HD), lambda h: (block, h))
    per_row = pl.BlockSpec((1, 1, rows), lambda h: (h, 0, block))
    out_head = pl.BlockSpec((rows, HD), lambda h: (0, h))
    sum_head = out_head if dq_sum is not None and dq_sum.shape[0] == rows else per_head
    sum_specs = ([] if dq_sum is None else [sum_head]) + (
        [] if dkv_sums is None else [whole((length, 2 * HD))] * n
    )
    return pl.pallas_call(
        body,
        grid=(heads,),
        in_specs=[smem, smem, per_head, per_head, per_row, per_row]
        + [whole((length, 2 * HD))] * n
        + sum_specs,
        out_specs=[out_head] + [whole((length, 2 * HD))] * n,
        out_shape=[jax.ShapeDtypeStruct((rows, cols), dq_type)]
        + [jax.ShapeDtypeStruct((length, 2 * HD), dkv_type)] * n,
        scratch_shapes=[
            pltpu.VMEM((n, HD, length), jnp.bfloat16),
            pltpu.VMEM((n, length, 2 * HD), jnp.float32),
        ],
        compiler_params=pltpu.CompilerParams(
            vmem_limit_bytes=32 * 2**20, dimension_semantics=("arbitrary",)
        ),
        cost_estimate=pl.CostEstimate(
            flops=10 * rows * length * n * cols,
            bytes_accessed=n * length * HD * 12 + rows * cols * 8,
            transcendentals=rows * length * n * heads,
        ),
    )(query_spans, key_spans, query, grad_out, lse2, delta, *kvs, *sums)


def prepare(pieces, out_heads, mine):
    rows, cols = pieces[0].shape
    heads = cols // HD

    def body(mine_ref, *refs):
        out_ref, grad_ref, delta_ref = refs[4:]
        for d in range(4):
            at = pl.ds(d * rows, rows)
            there = pl.ds(pl.multiple_of(mine_ref[d] * rows, rows), rows)
            grad_ref[at, :] = refs[d][...]
            for h in range(heads):
                cs = slice(h * HD, (h + 1) * HD)
                product = refs[d][:, cs].astype(jnp.float32) * out_ref[there, cs].astype(jnp.float32)
                delta_ref[h, :, at] = jnp.sum(product.T, axis=0, keepdims=True)

    vmem = pl.BlockSpec(memory_space=pltpu.VMEM)
    return pl.pallas_call(
        body,
        in_specs=[pl.BlockSpec(memory_space=pltpu.SMEM)] + [vmem] * 5,
        out_specs=[vmem, vmem],
        out_shape=[
            jax.ShapeDtypeStruct((4 * rows, cols), jnp.bfloat16),
            jax.ShapeDtypeStruct((heads, 1, 4 * rows), jnp.float32),
        ],
        compiler_params=pltpu.CompilerParams(vmem_limit_bytes=24 * 2**20),
        cost_estimate=pl.CostEstimate(
            flops=8 * rows * cols, bytes_accessed=24 * rows * cols, transcendentals=0
        ),
    )(mine, *pieces, out_heads)


def by_head(pieces, mine, widths):
    rows = pieces[0].shape[0]
    n = len(widths)

    def body(mine_ref, *refs):
        for d in range(4):
            at = 0
            for out_ref, width in zip(refs[4:], widths):
                to = pl.ds(pl.multiple_of(mine_ref[d] * width, HD), width)
                out_ref[:, to] = refs[d][:, at : at + width]
                at += width

    vmem = pl.BlockSpec(memory_space=pltpu.VMEM)
    return pl.pallas_call(
        body,
        in_specs=[pl.BlockSpec(memory_space=pltpu.SMEM)] + [vmem] * 4,
        out_specs=[vmem] * n,
        out_shape=[jax.ShapeDtypeStruct((rows, 4 * width), jnp.bfloat16) for width in widths],
        cost_estimate=pl.CostEstimate(
            flops=0, bytes_accessed=16 * rows * sum(widths), transcendentals=0
        ),
    )(mine, *pieces)


def shift(block, axis, by):
    size = lax.axis_size(axis)
    return lax.ppermute(block, axis, [(i, (i + by) % size) for i in range(size)])


def to_peer(block, d):
    return lax.ppermute(block, HEAD, [(i, i ^ d) for i in range(4)]) if d else block


def fence(*arrays):
    return lax.optimization_barrier(arrays)


def gather(blocks):
    half = blocks[0].shape[0] // 2
    axes = (("z", "x"), ("x", "z"))

    def step(sends):
        got = fence(*(shift(array, axis, by) for array, axis, by in sends))
        return list(zip(got[0::2], got[1::2]))

    block = [
        jnp.concatenate([b[s * half : (s + 1) * half] for b in blocks], axis=0) for s in range(2)
    ]
    near = step([(block[s], axes[s][0], by) for s in range(2) for by in (1, 3)])
    far = step(
        [
            (piece, axes[s][0], by)
            for s in range(2)
            for by, piece in ((1, near[s][0][:half]), (3, near[s][1][half:]))
        ]
    )
    line = [
        jnp.concatenate([block[s], near[s][0], far[s][0], far[s][1], near[s][1]], axis=0)
        for s in range(2)
    ]
    near = step([(line[s], axes[s][1], by) for s in range(2) for by in (1, 3)])
    far = step(
        [
            (piece, axes[s][1], by)
            for s in range(2)
            for by, piece in ((1, near[s][0][: 4 * half]), (3, near[s][1][4 * half :]))
        ]
    )
    return [[line[s], near[s][0], far[s][0], far[s][1], near[s][1]] for s in range(2)]


def lines_place(half):
    def copies(px, py, pz):
        for dx in range(4):
            for other in range(2):
                for dz in range(4):
                    for side, (first, second) in enumerate(((dz, dx), (dx, dz))):
                        src = (first * 2 + other) * half
                        kind = (0, 1, 2, 4)[second]
                        if second == 2 and first >= 2:
                            kind, src = 3, src - 4 * half
                        row = ((((px + 4 - dx) % 4) * 2 + (py + other) % 2) * 4 + (pz + 4 - dz) % 4)
                        yield dx, side * 5 + kind, src, row * (2 * half) + side * half, half

    return copies


def planes_place(length):
    def copies(px, py, pz):
        for dx in range(4):
            ax = (px + 4 - dx) % 4
            for z in range(4):
                for other in range(2):
                    src = ((ax * 4 + z) * 2 + other) * length
                    yield dx, 0, src, ((ax * 2 + (py + other) % 2) * 4 + z) * length, length

    return copies


def project(x_pieces, w_place, w_pieces, where):
    depth = x_pieces[0].shape[1]
    width = w_pieces[0].shape[1]
    chunk = depth // 4
    rows = sum(piece.shape[0] for piece in x_pieces)
    n_x, n_w = len(x_pieces), len(w_pieces)
    at_once = 512

    def body(where_ref, *refs):
        x_refs, w_refs = refs[:n_x], refs[n_x : n_x + n_w]
        out_ref, x_mem, w_mem, total, x_sems, w_sems = refs[n_x + n_w :]
        px, py, pz = where_ref[0], where_ref[1], where_ref[2]

        def columns(dx):
            return pl.ds(pl.multiple_of(((px + 4 - dx) % 4) * chunk, 128), chunk)

        moves = list(w_place(px, py, pz))
        for dx in range(4):
            for which, src, dst, size in [m[1:] for m in moves if m[0] == dx]:
                src = src if isinstance(src, int) else pl.multiple_of(src, 16)
                pltpu.make_async_copy(
                    w_refs[which].at[pl.ds(src, size), :],
                    w_mem.at[pl.ds(pl.multiple_of(dst, 16), size), :],
                    w_sems.at[dx],
                ).start()
            at = 0
            for ref in x_refs:
                pltpu.make_async_copy(
                    ref.at[:, columns(dx)],
                    x_mem.at[pl.ds(at, ref.shape[0]), columns(dx)],
                    x_sems.at[dx],
                ).start()
                at += ref.shape[0]
        for dx in range(4):
            here = columns(dx)
            pltpu.make_async_copy(w_mem.at[here, :], w_mem.at[here, :], w_sems.at[dx]).wait()
            pltpu.make_async_copy(x_mem.at[:, here], x_mem.at[:, here], x_sems.at[dx]).wait()
            for start in range(0, rows, at_once):
                at = pl.ds(start, at_once)
                part = dot(x_mem[at, here], w_mem[here, :], NN)
                if dx == 0:
                    total[at, :] = part
                elif dx == 3:
                    out_ref[at, :] = (total[at, :] + part).astype(jnp.bfloat16)
                else:
                    total[at, :] += part

    hbm = pl.BlockSpec(memory_space=pltpu.HBM)
    return pl.pallas_call(
        body,
        in_specs=[pl.BlockSpec(memory_space=pltpu.SMEM)] + [hbm] * (n_x + n_w),
        out_specs=pl.BlockSpec(memory_space=pltpu.VMEM),
        out_shape=jax.ShapeDtypeStruct((rows, width), jnp.bfloat16),
        scratch_shapes=[
            pltpu.VMEM((rows, depth), jnp.bfloat16),
            pltpu.VMEM((depth, width), jnp.bfloat16),
            pltpu.VMEM((rows, width), jnp.float32),
            pltpu.SemaphoreType.DMA((4,)),
            pltpu.SemaphoreType.DMA((4,)),
        ],
        compiler_params=pltpu.CompilerParams(vmem_limit_bytes=56 * 2**20),
        cost_estimate=pl.CostEstimate(
            flops=2 * rows * depth * width,
            bytes_accessed=2 * (rows * depth + depth * width + rows * width),
            transcendentals=0,
        ),
    )(where, *x_pieces, *w_pieces)


def local(x_ckpt, w_query, w_key, w_value, dout_seq, out_heads, lse_heads, span_order):
    rows = x_ckpt.shape[0]
    cols = w_query.shape[1]
    me = lax.axis_index(HEAD)
    group = lax.axis_index(BLK)
    groups = lax.axis_size(BLK)
    peers = range(4)
    mine = [me ^ d for d in peers]
    mine_all = jnp.stack(mine)
    where = jnp.stack([lax.axis_index(axis) for axis in ("x", "y_hi", "z")])

    w_own = jnp.concatenate([w_key, w_value, w_query], axis=1)
    w_pair = shift(w_own, "y_hi", 1)
    q_rows = jnp.concatenate([w_query, w_pair[:, 2 * HD :]], axis=0)
    q_weights = lax.all_gather(q_rows, ("x", "z"), axis=0, tiled=True)
    kv_lines = gather([w_own[:, : 2 * HD], w_pair[:, : 2 * HD]])

    x_sent, _ = fence(x_ckpt, w_pair)
    x_far = to_peer(x_sent, 2)
    x_core = to_peer(x_sent, 1)
    x_far, *flat = fence(x_far, *kv_lines[0], *kv_lines[1])
    kv_lines = [flat[:5], flat[5:]]
    x_pieces = [x_ckpt, x_core, x_far, to_peer(x_far, 1)]

    lse_rows = lse_heads.T * LOG2E
    lse2 = jnp.concatenate(
        [lax.dynamic_slice_in_dim(lse_rows, mine[d] * rows, rows, 1) for d in peers], axis=1
    )[:, None, :]
    spans = rows // SPAN

    def spans_of(which):
        base = which * (4 * spans)
        return jnp.concatenate(
            [lax.dynamic_slice_in_dim(span_order, base + mine[d] * spans, spans) for d in peers]
        )

    span_ids = [spans_of((group - r) % groups) for r in range(REACH + 1)]

    kv = project(x_pieces, lines_place(w_own.shape[0] // 2), kv_lines[0] + kv_lines[1], where)
    kv1 = shift(kv, BLK, 1)
    grads = [lax.dynamic_slice_in_dim(dout_seq, mine[d] * cols, cols, 1) for d in peers]
    *grads, _ = fence(*grads, x_far)
    grads = [to_peer(grads[d], d) for d in peers]
    query = project(x_pieces, planes_place(w_query.shape[0]), [q_weights], where)
    *grads, query = fence(*grads, query)
    grad_out, delta = prepare(grads, out_heads, mine_all)
    kv1, delta = fence(kv1, delta)
    kv2 = shift(kv1, BLK, 1)

    def part(start, count, keys, ids, own, dq_sum, dkv_sum, dq_type, dkv_type):
        return tile_grads(
            start, count, query, grad_out, lse2, delta, span_ids[0], ids[None], [keys], own,
            dq_sum, None if dkv_sum is None else [dkv_sum], dq_type, dkv_type,
        )

    f32, bf16 = jnp.float32, jnp.bfloat16
    half = 2 * rows
    dq, dkv1 = part(0, 4 * rows, kv1, span_ids[1], -1, None, None, f32, bf16)
    back1 = shift(dkv1, BLK, -1)
    dq, dkv2 = part(0, 4 * rows, kv2, span_ids[2], -1, dq, None, f32, bf16)
    back2 = shift(dkv2, BLK, -2)
    dq_far, dkv0 = part(half, half, kv, span_ids[0], 0, dq, None, bf16, f32)
    dq2, dq3 = to_peer(dq_far[:rows], 2), to_peer(dq_far[rows:], 3)
    dq_near, dkv0 = part(0, half, kv, span_ids[0], 0, dq, dkv0, bf16, f32)
    dq1 = to_peer(dq_near[rows:], 1)
    dkv = (dkv0 + back1.astype(f32) + back2.astype(f32)).astype(bf16)
    dkv, dq2, dq3 = fence(dkv, dq2, dq3)
    dkvs = [to_peer(dkv[d * rows : (d + 1) * rows], d) for d in peers]
    (grad_query,) = by_head([dq_near[:rows], dq1, dq2, dq3], mine_all, [cols])
    grad_key, grad_value = by_head(dkvs, mine_all, [HD, HD])
    return grad_query, grad_key, grad_value


def solution(mesh):
    fine = Mesh(mesh.devices.reshape(FINE), HEAD + BLK)
    rows = P(BLK + HEAD, None)
    both = P(BLK, HEAD)
    return jax.shard_map(
        local,
        mesh=fine,
        in_specs=(rows, both, both, both, rows, both, both, P()),
        out_specs=(rows, rows, rows),
        check_vma=False,
    )
```

```python
import jax
import jax.numpy as jnp
from jax import lax
from jax.experimental import pallas as pl
from jax.experimental.pallas import tpu as pltpu
from jax.sharding import Mesh, PartitionSpec as P

HD = 128
SPAN = 128
REACH = 2
HEAD = ("y_lo", "core")
BLK = ("x", "y_hi", "z")
FINE = (2, 2, 4, 2, 4)
SCALE = HD ** (-0.5)
LOG2E = 1.4426950408889634
BIG = 1e30
NN = (((1,), (0,)), ((), ()))
NT = (((1,), (1,)), ((), ()))


def dot(a, b, dims):
    return lax.dot_general(a, b, dims, preferred_element_type=jnp.float32)


def tile_grads(start, rows, query, grad_out, lse2, delta, query_spans, key_spans, kvs, own, dq_sum, dkv_sums, dq_type, dkv_type):
    cols = query.shape[1]
    heads = cols // HD
    n = len(kvs)
    length = kvs[0].shape[0]
    query_rows = min(256, rows)
    block = start // rows
    key_rows = length
    sums = ([] if dq_sum is None else [dq_sum]) + ([] if dkv_sums is None else list(dkv_sums))

    def body(qspan_ref, kspan_ref, q_ref, g_ref, lse_ref, delta_ref, *rest):
        kv_refs, rest = rest[:n], list(rest[n:])
        dq_sum_ref = rest.pop(0) if dq_sum is not None else None
        dkv_sum_refs = [rest.pop(0) for _ in range(n)] if dkv_sums is not None else None
        dq_ref, dkv_refs, kt_ref, total = rest[0], rest[1 : n + 1], rest[n + 1], rest[n + 2]

        @pl.when(pl.program_id(0) == 0)
        def _():
            for i in range(n):
                if dkv_sums is None:
                    total[i] = jnp.zeros((length, 2 * HD), jnp.float32)
                else:
                    total[i] = dkv_sum_refs[i][...]
                kt_ref[i] = kv_refs[i][:, :HD].T

        lane = lax.broadcasted_iota(jnp.int32, (1, query_rows), 1)
        spans = query_rows // SPAN
        for qb in range(rows // query_rows):
            qs = pl.ds(qb * query_rows, query_rows)
            q, g = q_ref[qs, :], g_ref[qs, :]
            lse, delt = lse_ref[0, :, qs], delta_ref[0, :, qs]
            qspan = jnp.full((1, query_rows), qspan_ref[start // SPAN + qb * spans], jnp.int32)
            for s in range(1, spans):
                qspan = jnp.where(lane >= s * SPAN, qspan_ref[start // SPAN + qb * spans + s], qspan)
            qpos = qspan * SPAN + lane % SPAN
            dq = None
            for i in range(n):
                for kb in range(length // key_rows):
                    ks = pl.ds(kb * key_rows, key_rows)
                    score = dot(kv_refs[i][ks, :HD], q, NT)
                    gprob = dot(kv_refs[i][ks, HD:], g, NT)
                    probs, scores = [], []
                    for s in range(key_rows // SPAN):
                        at = slice(s * SPAN, (s + 1) * SPAN)
                        kspan = kspan_ref[i, kb * (key_rows // SPAN) + s]
                        if i == own:
                            kpos = kspan * SPAN + lax.broadcasted_iota(jnp.int32, (SPAN, 1), 0)
                            prob = jnp.exp2(
                                jnp.where(kpos <= qpos, score[at] * (SCALE * LOG2E) - lse, -BIG)
                            )
                        else:
                            prob = jnp.exp2(
                                score[at] * (SCALE * LOG2E) - jnp.where(kspan < qspan, lse, BIG)
                            )
                        probs.append(prob.astype(jnp.bfloat16))
                        scores.append((prob * (gprob[at] - delt)).astype(jnp.bfloat16))
                    prob_half = jnp.concatenate(probs, 0)
                    score_half = jnp.concatenate(scores, 0)
                    total[i, ks, HD:] += dot(prob_half, g, NN)
                    total[i, ks, :HD] += dot(score_half, q, NN) * SCALE
                    part = dot(kt_ref[i, :, ks], score_half, NN)
                    dq = part if dq is None else dq + part
            dq = dq.T * SCALE
            if dq_sum is not None:
                dq = dq + dq_sum_ref[qs, :]
            dq_ref[qs, :] = dq.astype(dq_type)

        @pl.when(pl.program_id(0) == heads - 1)
        def _():
            for i in range(n):
                dkv_refs[i][...] = total[i].astype(dkv_type)

    def whole(shape):
        return pl.BlockSpec(shape, lambda h: (0,) * len(shape))

    smem = pl.BlockSpec(memory_space=pltpu.SMEM)
    per_head = pl.BlockSpec((rows, HD), lambda h: (block, h))
    per_row = pl.BlockSpec((1, 1, rows), lambda h: (h, 0, block))
    out_head = pl.BlockSpec((rows, HD), lambda h: (0, h))
    sum_head = out_head if dq_sum is not None and dq_sum.shape[0] == rows else per_head
    sum_specs = ([] if dq_sum is None else [sum_head]) + (
        [] if dkv_sums is None else [whole((length, 2 * HD))] * n
    )
    return pl.pallas_call(
        body,
        grid=(heads,),
        in_specs=[smem, smem, per_head, per_head, per_row, per_row]
        + [whole((length, 2 * HD))] * n
        + sum_specs,
        out_specs=[out_head] + [whole((length, 2 * HD))] * n,
        out_shape=[jax.ShapeDtypeStruct((rows, cols), dq_type)]
        + [jax.ShapeDtypeStruct((length, 2 * HD), dkv_type)] * n,
        scratch_shapes=[
            pltpu.VMEM((n, HD, length), jnp.bfloat16),
            pltpu.VMEM((n, length, 2 * HD), jnp.float32),
        ],
        compiler_params=pltpu.CompilerParams(
            vmem_limit_bytes=32 * 2**20, dimension_semantics=("arbitrary",)
        ),
        cost_estimate=pl.CostEstimate(
            flops=10 * rows * length * n * cols,
            bytes_accessed=n * length * HD * 12 + rows * cols * 8,
            transcendentals=rows * length * n * heads,
        ),
    )(query_spans, key_spans, query, grad_out, lse2, delta, *kvs, *sums)


def prepare(pieces, out_heads, mine):
    rows, cols = pieces[0].shape
    heads = cols // HD

    def body(mine_ref, *refs):
        out_ref, grad_ref, delta_ref = refs[4:]
        for d in range(4):
            at = pl.ds(d * rows, rows)
            there = pl.ds(pl.multiple_of(mine_ref[d] * rows, rows), rows)
            grad_ref[at, :] = refs[d][...]
            for h in range(heads):
                cs = slice(h * HD, (h + 1) * HD)
                product = refs[d][:, cs].astype(jnp.float32) * out_ref[there, cs].astype(jnp.float32)
                delta_ref[h, :, at] = jnp.sum(product.T, axis=0, keepdims=True)

    vmem = pl.BlockSpec(memory_space=pltpu.VMEM)
    return pl.pallas_call(
        body,
        in_specs=[pl.BlockSpec(memory_space=pltpu.SMEM)] + [vmem] * 5,
        out_specs=[vmem, vmem],
        out_shape=[
            jax.ShapeDtypeStruct((4 * rows, cols), jnp.bfloat16),
            jax.ShapeDtypeStruct((heads, 1, 4 * rows), jnp.float32),
        ],
        compiler_params=pltpu.CompilerParams(vmem_limit_bytes=24 * 2**20),
        cost_estimate=pl.CostEstimate(
            flops=8 * rows * cols, bytes_accessed=24 * rows * cols, transcendentals=0
        ),
    )(mine, *pieces, out_heads)


def by_head(pieces, mine, widths):
    rows = pieces[0].shape[0]
    n = len(widths)

    def body(mine_ref, *refs):
        for d in range(4):
            at = 0
            for out_ref, width in zip(refs[4:], widths):
                to = pl.ds(pl.multiple_of(mine_ref[d] * width, HD), width)
                out_ref[:, to] = refs[d][:, at : at + width]
                at += width

    vmem = pl.BlockSpec(memory_space=pltpu.VMEM)
    return pl.pallas_call(
        body,
        in_specs=[pl.BlockSpec(memory_space=pltpu.SMEM)] + [vmem] * 4,
        out_specs=[vmem] * n,
        out_shape=[jax.ShapeDtypeStruct((rows, 4 * width), jnp.bfloat16) for width in widths],
        cost_estimate=pl.CostEstimate(
            flops=0, bytes_accessed=16 * rows * sum(widths), transcendentals=0
        ),
    )(mine, *pieces)


def sum_pieces(total, *parts):
    rows, cols = total.shape[0] // 4, total.shape[1]

    def body(*refs):
        for d in range(4):
            at = pl.ds(d * rows, rows)
            result = refs[0][at, :]
            for ref in refs[1 : 1 + len(parts)]:
                result = result + ref[at, :].astype(jnp.float32)
            refs[1 + len(parts) + d][...] = result.astype(jnp.bfloat16)

    vmem = pl.BlockSpec(memory_space=pltpu.VMEM)
    return pl.pallas_call(
        body,
        in_specs=[vmem] * (1 + len(parts)),
        out_specs=[vmem] * 4,
        out_shape=[jax.ShapeDtypeStruct((rows, cols), jnp.bfloat16)] * 4,
        compiler_params=pltpu.CompilerParams(vmem_limit_bytes=16 * 2**20),
        cost_estimate=pl.CostEstimate(
            flops=8 * rows * cols, bytes_accessed=40 * rows * cols, transcendentals=0
        ),
    )(total, *parts)


def shift(block, axis, by):
    size = lax.axis_size(axis)
    return lax.ppermute(block, axis, [(i, (i + by) % size) for i in range(size)])


def to_peer(block, d):
    return lax.ppermute(block, HEAD, [(i, i ^ d) for i in range(4)]) if d else block


def fence(*arrays):
    return lax.optimization_barrier(arrays)


def gather(blocks):
    half = blocks[0].shape[0] // 2
    axes = (("z", "x"), ("x", "z"))

    def step(sends):
        got = fence(*(shift(array, axis, by) for array, axis, by in sends))
        return list(zip(got[0::2], got[1::2]))

    block = [
        jnp.concatenate([b[s * half : (s + 1) * half] for b in blocks], axis=0) for s in range(2)
    ]
    near = step([(block[s], axes[s][0], by) for s in range(2) for by in (1, 3)])
    far = step(
        [
            (piece, axes[s][0], by)
            for s in range(2)
            for by, piece in ((1, near[s][0][:half]), (3, near[s][1][half:]))
        ]
    )
    line = [
        jnp.concatenate([block[s], near[s][0], far[s][0], far[s][1], near[s][1]], axis=0)
        for s in range(2)
    ]
    near = step([(line[s], axes[s][1], by) for s in range(2) for by in (1, 3)])
    far = step(
        [
            (piece, axes[s][1], by)
            for s in range(2)
            for by, piece in ((1, near[s][0][: 4 * half]), (3, near[s][1][4 * half :]))
        ]
    )
    return [[line[s], near[s][0], far[s][0], far[s][1], near[s][1]] for s in range(2)]


def lines_place(half):
    def copies(px, py, pz):
        for dx in range(4):
            for other in range(2):
                for dz in range(4):
                    for side, (first, second) in enumerate(((dz, dx), (dx, dz))):
                        src = (first * 2 + other) * half
                        kind = (0, 1, 2, 4)[second]
                        if second == 2 and first >= 2:
                            kind, src = 3, src - 4 * half
                        row = ((((px + 4 - dx) % 4) * 2 + (py + other) % 2) * 4 + (pz + 4 - dz) % 4)
                        yield dx, side * 5 + kind, src, row * (2 * half) + side * half, half

    return copies


def planes_place(length):
    def copies(px, py, pz):
        for dx in range(4):
            ax = (px + 4 - dx) % 4
            for z in range(4):
                for other in range(2):
                    src = ((ax * 4 + z) * 2 + other) * length
                    yield dx, 0, src, ((ax * 2 + (py + other) % 2) * 4 + z) * length, length

    return copies


def project(x_pieces, w_place, w_pieces, where):
    depth = x_pieces[0].shape[1]
    width = w_pieces[0].shape[1]
    chunk = depth // 4
    rows = sum(piece.shape[0] for piece in x_pieces)
    n_x, n_w = len(x_pieces), len(w_pieces)
    at_once = 512

    def body(where_ref, *refs):
        x_refs, w_refs = refs[:n_x], refs[n_x : n_x + n_w]
        out_ref, x_mem, w_mem, total, x_sems, w_sems = refs[n_x + n_w :]
        px, py, pz = where_ref[0], where_ref[1], where_ref[2]

        def columns(dx):
            return pl.ds(pl.multiple_of(((px + 4 - dx) % 4) * chunk, 128), chunk)

        moves = list(w_place(px, py, pz))
        for dx in range(4):
            for which, src, dst, size in [m[1:] for m in moves if m[0] == dx]:
                src = src if isinstance(src, int) else pl.multiple_of(src, 16)
                pltpu.make_async_copy(
                    w_refs[which].at[pl.ds(src, size), :],
                    w_mem.at[pl.ds(pl.multiple_of(dst, 16), size), :],
                    w_sems.at[dx],
                ).start()
            at = 0
            for ref in x_refs:
                pltpu.make_async_copy(
                    ref.at[:, columns(dx)],
                    x_mem.at[pl.ds(at, ref.shape[0]), columns(dx)],
                    x_sems.at[dx],
                ).start()
                at += ref.shape[0]
        for dx in range(4):
            here = columns(dx)
            pltpu.make_async_copy(w_mem.at[here, :], w_mem.at[here, :], w_sems.at[dx]).wait()
            pltpu.make_async_copy(x_mem.at[:, here], x_mem.at[:, here], x_sems.at[dx]).wait()
            for start in range(0, rows, at_once):
                at = pl.ds(start, at_once)
                part = dot(x_mem[at, here], w_mem[here, :], NN)
                if dx == 0:
                    total[at, :] = part
                elif dx == 3:
                    out_ref[at, :] = (total[at, :] + part).astype(jnp.bfloat16)
                else:
                    total[at, :] += part

    hbm = pl.BlockSpec(memory_space=pltpu.HBM)
    return pl.pallas_call(
        body,
        in_specs=[pl.BlockSpec(memory_space=pltpu.SMEM)] + [hbm] * (n_x + n_w),
        out_specs=pl.BlockSpec(memory_space=pltpu.VMEM),
        out_shape=jax.ShapeDtypeStruct((rows, width), jnp.bfloat16),
        scratch_shapes=[
            pltpu.VMEM((rows, depth), jnp.bfloat16),
            pltpu.VMEM((depth, width), jnp.bfloat16),
            pltpu.VMEM((rows, width), jnp.float32),
            pltpu.SemaphoreType.DMA((4,)),
            pltpu.SemaphoreType.DMA((4,)),
        ],
        compiler_params=pltpu.CompilerParams(vmem_limit_bytes=56 * 2**20),
        cost_estimate=pl.CostEstimate(
            flops=2 * rows * depth * width,
            bytes_accessed=2 * (rows * depth + depth * width + rows * width),
            transcendentals=0,
        ),
    )(where, *x_pieces, *w_pieces)


def local(x_ckpt, w_query, w_key, w_value, dout_seq, out_heads, lse_heads, span_order):
    rows = x_ckpt.shape[0]
    cols = w_query.shape[1]
    me = lax.axis_index(HEAD)
    group = lax.axis_index(BLK)
    groups = lax.axis_size(BLK)
    peers = range(4)
    mine = [me ^ d for d in peers]
    mine_all = jnp.stack(mine)
    where = jnp.stack([lax.axis_index(axis) for axis in ("x", "y_hi", "z")])

    w_own = jnp.concatenate([w_key, w_value, w_query], axis=1)
    w_pair = shift(w_own, "y_hi", 1)
    q_rows = jnp.concatenate([w_query, w_pair[:, 2 * HD :]], axis=0)
    q_weights = lax.all_gather(q_rows, ("x", "z"), axis=0, tiled=True)
    kv_lines = gather([w_own[:, : 2 * HD], w_pair[:, : 2 * HD]])

    x_sent, _ = fence(x_ckpt, w_pair)
    x_far = to_peer(x_sent, 2)
    x_core = to_peer(x_sent, 1)
    x_far, *flat = fence(x_far, *kv_lines[0], *kv_lines[1])
    kv_lines = [flat[:5], flat[5:]]
    x_pieces = [x_ckpt, x_core, x_far, to_peer(x_far, 1)]

    lse_rows = lse_heads.T * LOG2E
    lse2 = jnp.concatenate(
        [lax.dynamic_slice_in_dim(lse_rows, mine[d] * rows, rows, 1) for d in peers], axis=1
    )[:, None, :]
    spans = rows // SPAN

    def spans_of(which):
        base = which * (4 * spans)
        return jnp.concatenate(
            [lax.dynamic_slice_in_dim(span_order, base + mine[d] * spans, spans) for d in peers]
        )

    span_ids = [spans_of((group - r) % groups) for r in range(REACH + 1)]

    kv = project(x_pieces, lines_place(w_own.shape[0] // 2), kv_lines[0] + kv_lines[1], where)
    kv1 = shift(kv, BLK, 1)
    grads = [lax.dynamic_slice_in_dim(dout_seq, mine[d] * cols, cols, 1) for d in peers]
    *grads, _ = fence(*grads, x_far)
    grads = [to_peer(grads[d], d) for d in peers]
    query = project(x_pieces, planes_place(w_query.shape[0]), [q_weights], where)
    *grads, query = fence(*grads, query)
    grad_out, delta = prepare(grads, out_heads, mine_all)
    kv1, delta = fence(kv1, delta)
    kv2 = shift(kv1, BLK, 1)

    def part(start, count, keys, ids, own, dq_sum, dkv_sum, dq_type, dkv_type):
        return tile_grads(
            start, count, query, grad_out, lse2, delta, span_ids[0], ids[None], [keys], own,
            dq_sum, None if dkv_sum is None else [dkv_sum], dq_type, dkv_type,
        )

    f32, bf16 = jnp.float32, jnp.bfloat16
    half = 2 * rows
    dq, dkv1 = part(0, 4 * rows, kv1, span_ids[1], -1, None, None, f32, bf16)
    back1 = shift(dkv1, BLK, -1)
    dq, dkv2 = part(0, 4 * rows, kv2, span_ids[2], -1, dq, None, f32, bf16)
    back2 = shift(dkv2, BLK, -2)
    dq_far, dkv0 = part(half, half, kv, span_ids[0], 0, dq, None, bf16, f32)
    dq2, dq3 = to_peer(dq_far[:rows], 2), to_peer(dq_far[rows:], 3)
    dq_near, dkv0 = part(0, half, kv, span_ids[0], 0, dq, dkv0, bf16, f32)
    dq1 = to_peer(dq_near[rows:], 1)
    dkvs = sum_pieces(dkv0, back1, back2)
    *dkvs, dq2, dq3 = fence(*dkvs, dq2, dq3)
    dkvs = [to_peer(dkvs[d], d) for d in peers]
    (grad_query,) = by_head([dq_near[:rows], dq1, dq2, dq3], mine_all, [cols])
    grad_key, grad_value = by_head(dkvs, mine_all, [HD, HD])
    return grad_query, grad_key, grad_value


def solution(mesh):
    fine = Mesh(mesh.devices.reshape(FINE), HEAD + BLK)
    rows = P(BLK + HEAD, None)
    both = P(BLK, HEAD)
    return jax.shard_map(
        local,
        mesh=fine,
        in_specs=(rows, both, both, both, rows, both, both, P()),
        out_specs=(rows, rows, rows),
        check_vma=False,
    )
```
